32 devices in a mesh: groups: 2 (over x), row: 16 (over z, y, core).
Axes of the slice: x: 2, y: 2, z: 4, core: 2. Of those that a mesh axis runs over, the one named last changes fastest.
Arguments:
- tokens: bfloat16 [2048, 5120], P(('groups', 'row')), parts along dimension 0, may hold values from -6 to 6
- w_query: bfloat16 [5120, 2048], P(None, 'row'), may hold values from -0.078125 to 0.078125
- w_key: bfloat16 [5120, 256], P(None, 'row'), may hold values from -0.078125 to 0.078125
- w_value: bfloat16 [5120, 256], P(None, 'row'), may hold values from -0.078125 to 0.078125
- q_gain: float32 [16, 128], P('row'), may hold values from 0.1 to 1.9
- k_gain: float32 [2, 128], replicated, may hold values from 0.1 to 1.9
Outputs:
- attended: bfloat16 [2048, 2048], P('groups', 'row'), parts along dimension 0
The draws below stay inside these ranges and needn't reach their ends.
There are 2 independent parts, one for each index of `groups`. The reference program is written for one: setup_inputs(seed, part) draws one part's arguments, and reference() takes and returns one part's arrays. A program takes and returns all parts, laid end to end along the dimension named above; an argument that names none is the same for every part. Nothing has to cross between parts.
All inputs are finite; a program needn't handle non-finite values.
Results may differ from the reference program's by a relative error of at most 0.0082.
Values may be sent and summed in bfloat16 or wider, within the bound.
A program may use at most 128 MiB of HBM per device.

```python
import jax
import jax.numpy as jnp
from jax import lax

D = 5120
HD = 128
GROUP = 8
HQ = 16
KVH = 2
TOKENS = 1024


def block_levels(stream_key, extent, shards, least, high):
    def one(dim, parts):
        draws = jax.random.uniform(jax.random.fold_in(jax.random.fold_in(stream_key, 6), dim), (parts,), jnp.float32, least / len(shards), high / len(shards))
        return jnp.repeat(jnp.exp(draws), extent[dim] // parts).reshape((-1,) + (1,) * (len(extent) - dim - 1))

    level = one(*shards[0])
    for cut in shards[1:]:
        level = level * one(*cut)
    return level


def noise(rng, dims, scale, reach, cuts=(), kind=jnp.bfloat16):
    factor_of = block_levels(rng, dims, cuts, -0.22, 0.18) if cuts else 1.0
    values = jax.random.normal(rng, dims, jnp.float32) * scale * factor_of
    return jnp.minimum(jnp.maximum(values, -reach), reach).astype(kind)


def setup_inputs(seed: int = 0, part: int = 0) -> dict:
    keys = jax.random.split(jax.random.key(seed), 7)
    own_keys = jax.random.split(jax.random.fold_in(keys[6], part), 7)
    return {
        "tokens": noise(own_keys[0], (TOKENS, D), 1.0, 6.0, ((0, 16),)),
        "w_query": noise(keys[1], (D, HQ * HD), D ** -0.5, 0.078125, ((1, 16),)),
        "w_key": noise(keys[2], (D, KVH * HD), D ** -0.5, 0.078125, ((1, 16),)),
        "w_value": noise(keys[3], (D, KVH * HD), D ** -0.5, 0.078125, ((1, 16),)),
        "q_gain": jnp.clip(1.0 + 0.18 * jax.random.normal(keys[4], (HQ, HD), jnp.float32), 0.1, 1.9),
        "k_gain": jnp.clip(1.0 + 0.18 * jax.random.normal(keys[5], (KVH, HD), jnp.float32), 0.1, 1.9),
    }


EPS = 1e-06
THETA = 1000000.0

def rope_tables(count, width):
    half = width // 2
    freq = THETA ** (-(jnp.arange(half, dtype=jnp.float32) * 2.0 / width))
    angles = jnp.arange(count, dtype=jnp.float32)[:, None] * freq[None, :]
    cosine = jnp.cos(angles)
    sine = jnp.sin(angles)
    return (jnp.concatenate([cosine, cosine], 1), jnp.concatenate([sine, sine], 1))

def norm_rope(raw, gain, cosine, sine):
    values = raw.astype(jnp.float32)
    scale = lax.rsqrt(lax.optimization_barrier(jnp.mean(values * values, -1, keepdims=True)) + EPS)
    normed = values * scale * gain.astype(jnp.float32)
    half = normed.shape[-1] // 2
    turned = jnp.concatenate([-normed[:, half:], normed[:, :half]], 1)
    return (normed * cosine + turned * sine).astype(jnp.bfloat16)

def attend(query, start, key, value):
    width = query.shape[1]
    scores = jnp.dot(query, key.T, preferred_element_type=jnp.float32) * float(width) ** (-0.5)
    rows = start + lax.broadcasted_iota(jnp.int32, scores.shape, 0)
    cols = lax.broadcasted_iota(jnp.int32, scores.shape, 1)
    scores = jnp.where(cols <= rows, scores, jnp.float32(-1e+30))
    top = lax.optimization_barrier(jnp.max(scores, -1, keepdims=True))
    weights = jnp.exp(scores - top)
    total = lax.optimization_barrier(jnp.sum(weights, -1, keepdims=True))
    probs = (weights / total).astype(jnp.bfloat16)
    return jnp.dot(probs, value, preferred_element_type=jnp.float32).astype(jnp.bfloat16)

def reference(tokens, w_query, w_key, w_value, q_gain, k_gain):
    q_all = jnp.dot(tokens, w_query, preferred_element_type=jnp.float32).astype(jnp.bfloat16)
    k_all = jnp.dot(tokens, w_key, preferred_element_type=jnp.float32).astype(jnp.bfloat16)
    v_all = jnp.dot(tokens, w_value, preferred_element_type=jnp.float32).astype(jnp.bfloat16)
    cosine, sine = rope_tables(TOKENS, HD)

    def one_head(head):
        shared = head // GROUP
        query = lax.dynamic_slice_in_dim(q_all, head * HD, HD, 1)
        key = lax.dynamic_slice_in_dim(k_all, shared * HD, HD, 1)
        value = lax.dynamic_slice_in_dim(v_all, shared * HD, HD, 1)
        q_rot = norm_rope(query, lax.dynamic_slice_in_dim(q_gain, head, 1, 0), cosine, sine)
        k_rot = norm_rope(key, lax.dynamic_slice_in_dim(k_gain, shared, 1, 0), cosine, sine)
        return attend(q_rot, 0, k_rot, value)
    heads = lax.map(one_head, jnp.arange(HQ, dtype=jnp.int32))
    return jnp.transpose(heads, (1, 0, 2)).reshape(TOKENS, HQ * HD)
```

```python
import jax
import jax.numpy as jnp
from jax import lax
from jax.experimental import pallas as pl
from jax.experimental.pallas import tpu as pltpu
from jax.sharding import PartitionSpec as P

GROUP = 8


EPS = 1e-06
THETA = 1000000.0


def swapped(block, axis, apart):
    count = lax.axis_size(axis)
    route = []
    for low in range(count):
        high = low | 1 << apart
        if high != low and high < count:
            route += [(low, high), (high, low)]
    return lax.ppermute(block, axis, route)


def rope_tables(count, width):
    half = width // 2
    freq = THETA ** (-(jnp.arange(half, dtype=jnp.float32) * 2.0 / width))
    angles = jnp.arange(count, dtype=jnp.float32)[:, None] * freq[None, :]
    cosine = jnp.cos(angles)
    sine = jnp.sin(angles)
    return (jnp.concatenate([cosine, cosine], 1), jnp.concatenate([sine, sine], 1))


def norm_rope(raw, gain, cosine, sine):
    values = raw.astype(jnp.float32)
    scale = lax.rsqrt(jnp.mean(values * values, -1, keepdims=True) + EPS)
    normed = values * scale * gain
    half = normed.shape[-1] // 2
    turned = jnp.concatenate([-normed[:, half:], normed[:, :half]], 1)
    return (normed * cosine + turned * sine).astype(jnp.bfloat16)


def attend(query, start, key, value):
    width = query.shape[1]
    scores = jnp.dot(query, key.T, preferred_element_type=jnp.float32) * float(width) ** (-0.5)
    rows = start + lax.broadcasted_iota(jnp.int32, scores.shape, 0)
    cols = lax.broadcasted_iota(jnp.int32, scores.shape, 1)
    scores = jnp.where(cols <= rows, scores, jnp.float32(-1e30))
    top = jnp.max(scores, -1, keepdims=True)
    weights = jnp.exp(scores - top)
    total = jnp.sum(weights, -1, keepdims=True)
    probs = (weights / total).astype(jnp.bfloat16)
    return jnp.dot(probs, value, preferred_element_type=jnp.float32).astype(jnp.bfloat16)


def order_pair(mine, other, upper):
    lower_part = jnp.where(upper, other, mine)
    upper_part = jnp.where(upper, mine, other)
    return jnp.concatenate([lower_part, upper_part], 1)


def gathered_device(tokens, w_query, w_key, w_value, q_gain, k_gain):
    devices = lax.axis_size("row")
    owner = lax.axis_index("row")
    head_size = w_query.shape[1]
    count = tokens.shape[0] * devices
    shared = owner // GROUP
    levels = GROUP.bit_length() - 1
    merged = jnp.concatenate([w_query, w_key, w_value], 1)
    projected = jnp.dot(
        lax.all_gather(tokens, "row", axis=0, tiled=True),
        merged,
        preferred_element_type=jnp.float32,
    ).astype(jnp.bfloat16)
    query = projected[:, :head_size]
    key_cols = w_key.shape[1]
    key = projected[:, head_size : head_size + key_cols]
    value = projected[:, head_size + key_cols :]
    for level in range(levels):
        k_other, v_other = swapped((key, value), "row", level)
        upper = owner >> level & 1 == 1
        key = order_pair(key, k_other, upper)
        value = order_pair(value, v_other, upper)
    cosine, sine = rope_tables(count, head_size)
    q_rot = norm_rope(query, q_gain, cosine, sine)
    k_rot = norm_rope(key, lax.dynamic_slice_in_dim(k_gain, shared, 1, 0), cosine, sine)
    block = min(512, count)
    outputs = []
    for index in range(count // block):
        start = index * block
        finish = start + block
        outputs.append(attend(q_rot[start:finish], start, k_rot[:finish], value[:finish]))
    return jnp.concatenate(outputs, 0)


LINE, PLANE = 4, 4
CHUNKS = 4
PARTS = 8


def layer_kernel(
    tokens, w_query, w_kv_k, w_kv_v, q_gain, k_gain, freq, out,
    tok, wq, wkv, q_stage, q_all, kv_all, cos_t, sin_t, acc_q, acc_kv,
    local_sem, right_send, left_send, tok_recv,
    core_send, core_recv, y_send, x_send, w_recv, diag_send, diag_recv,
    q_send, q_recv, kv_send, kv_recv,
):
    me = lax.axis_index("row")
    g = lax.axis_index("groups")
    z, s = me // PLANE, me % PLANE
    y, c = s // 2, s % 2
    peers = [s, y * 2 + 1 - c, (1 - y) * 2 + c, (1 - y) * 2 + 1 - c]
    half = z % 2
    pair_z = z + 1 - 2 * half
    shared = z // 2
    rows, width = tokens.shape
    head = w_query.shape[1]
    step = width // CHUNKS
    part = width // PARTS

    def at(zz, ss):
        return {"row": zz * PLANE + ss}

    barrier = pltpu.get_barrier_semaphore()
    friends = [at(z, p) for p in peers[1:]] + [at(pair_z, p) for p in peers]
    friends.append({"groups": 1 - g})
    for friend in friends:
        pl.semaphore_signal(barrier, inc=1, device_id=friend)
    far_z = z - 1 + 2 * half
    has_far = jnp.logical_and(far_z >= 0, far_z < LINE)

    @pl.when(has_far)
    def _():
        pl.semaphore_signal(barrier, inc=1, device_id=at(far_z, s))

    def own(src, dst, index):
        return pltpu.make_async_copy(src, dst, local_sem.at[index])

    locals_ = [
        own(w_kv_k, wkv.at[0, s], 0),
        own(w_kv_v, wkv.at[1, s], 1),
        own(tokens, tok.at[z], 2),
        own(w_query, wq.at[:, pl.ds(0, head)], 3),
    ]
    for copy in locals_:
        copy.start()

    pl.semaphore_wait(barrier, len(friends) + jnp.where(has_far, 1, 0))

    def remote(src, dst, send, recv, device):
        return pltpu.make_async_remote_copy(src, dst, send, recv, device_id=device)

    def token_copy(block, chunk, right, src=None):
        view = tok.at[block, :, pl.ds(chunk * step, step)]
        sems = right_send if right else left_send
        return remote(
            view if src is None else src, view, sems.at[block, chunk],
            tok_recv.at[block, chunk], at(z + 1 if right else z - 1, s),
        )

    for chunk in range(CHUNKS):
        view = tokens.at[:, pl.ds(chunk * step, step)]

        @pl.when(z > 0)
        def _():
            token_copy(z, chunk, False, view).start()

        @pl.when(z < LINE - 1)
        def _():
            token_copy(z, chunk, True, view).start()

    last_piece = PARTS // 2

    def piece(i, parity, slot):
        if i == last_piece:
            return wkv.at[parity, peers[slot]], PARTS + parity
        index = 2 * i + parity
        rows_ = pl.ds(pl.multiple_of(index * part, part), part)
        return wq.at[rows_, pl.ds(slot * head, head)], index

    def y_copy(i):
        view, index = piece(i, g, 2)
        mine, _ = piece(i, g, 0)
        if i == last_piece:
            view = mine
        return remote(mine, view, y_send.at[i], w_recv.at[index], at(z, peers[2]))

    def y_arrival(i):
        view, index = piece(i, g, 2)
        return remote(view, view, y_send.at[i], w_recv.at[index], at(z, peers[2]))

    def x_copy(i, parity):
        view, index = piece(i, parity, 2)
        return remote(view, view, x_send.at[i], w_recv.at[index], {"groups": 1 - g})

    def diag_copy(i, parity):
        view, index = piece(i, parity, 2)
        if i == last_piece:
            there = view
        else:
            there, _ = piece(i, parity, 3)
        return remote(view, there, diag_send.at[index], diag_recv.at[index], at(z, peers[1]))

    def diag_arrival(i, parity):
        view, index = piece(i, parity, 3)
        return remote(view, view, diag_send.at[index], diag_recv.at[index], at(z, peers[1]))

    def core_copies(incoming):
        whose = peers[1] if incoming else s
        cols = pl.ds(head, head)
        mine = wq.at[:, cols] if incoming else wq.at[:, pl.ds(0, head)]
        return [
            remote(wkv.at[i, whose], wkv.at[i, whose], core_send.at[i], core_recv.at[i], at(z, peers[1]))
            for i in (0, 1)
        ] + [remote(mine, wq.at[:, cols], core_send.at[2], core_recv.at[2], at(z, peers[1]))]

    for copy in locals_:
        copy.wait()
    for i in range(last_piece + 1):
        y_copy(i).start()
    for copy in core_copies(False):
        copy.start()

    spot = lax.broadcasted_iota(jnp.int32, cos_t.shape, 0).astype(jnp.float32)
    angle = spot * freq[...]
    lane = lax.broadcasted_iota(jnp.int32, cos_t.shape, 1)
    cos_t[...] = jnp.cos(angle)
    sine = jnp.sin(angle)
    sin_t[...] = jnp.where(lane < head // 2, -sine, sine)

    def pass_on(distance, chunk):
        low, high = z - distance, z + distance

        @pl.when(low >= 0)
        def _():
            token_copy(low, chunk, True).wait_recv()

            @pl.when(z < LINE - 1)
            def _():
                token_copy(low, chunk, True).start()

        @pl.when(high < LINE)
        def _():
            token_copy(high, chunk, False).wait_recv()

            @pl.when(z > 0)
            def _():
                token_copy(high, chunk, False).start()

    def take_x(i):
        x_copy(i, 1 - g).wait_recv()
        diag_copy(i, 1 - g).start()

    for i in range(last_piece + 1):
        y_arrival(i).wait_recv()
        x_copy(i, g).start()
        diag_copy(i, g).start()
        if i < CHUNKS:
            pass_on(1, i)
        if i > 0:
            take_x(i - 1)
    take_x(last_piece)
    for copy in core_copies(True):
        copy.wait_recv()
    for i in range(last_piece + 1):
        diag_arrival(i, g).wait_recv()
        diag_arrival(i, 1 - g).wait_recv()

    def result_copies(block):
        place = block * PLANE + s
        copies = []
        for t in (1, 2, 3):
            copies.append(remote(
                q_stage.at[block, t - 1], q_all.at[place], q_send.at[block, t - 1],
                q_recv.at[block, t - 1], at(z, peers[t]),
            ))
        for far in (0, 1):
            for t in range(PLANE):
                if far == 0 and t == 0:
                    continue
                i = far * PLANE + t - 1
                copies.append(remote(
                    kv_all.at[half, place], kv_all.at[half, place], kv_send.at[block, i],
                    kv_recv.at[block, i], at(pair_z if far else z, peers[t]),
                ))
        return copies

    def result_arrivals(block):
        arrivals = []
        for t in (1, 2, 3):
            place = q_all.at[block * PLANE + peers[t]]
            arrivals.append(remote(
                place, place, q_send.at[block, t - 1], q_recv.at[block, t - 1], at(z, peers[t]),
            ))
        for far in (0, 1):
            for t in range(PLANE):
                if far == 0 and t == 0:
                    continue
                i = far * PLANE + t - 1
                place = kv_all.at[1 - half if far else half, block * PLANE + peers[t]]
                arrivals.append(remote(
                    place, place, kv_send.at[block, i], kv_recv.at[block, i],
                    at(pair_z if far else z, peers[t]),
                ))
        return arrivals

    def finish(block, q_sum, kv_sum):
        q_bf = q_sum.astype(jnp.bfloat16)
        place = block * PLANE + s
        q_all[place] = q_bf[:, :head]
        for t in (1, 2, 3):
            q_stage[block, t - 1] = q_bf[:, t * head : (t + 1) * head]
        kv_all[half, place] = kv_sum.astype(jnp.bfloat16)
        for copy in result_copies(block):
            copy.start()

    def products(block, cols):
        part_tok = tok[block, :, cols]
        q_part = jnp.dot(part_tok, wq[cols, :], preferred_element_type=jnp.float32)
        kv_w = wkv[:, :, :, cols]
        kv_w = kv_w.reshape(kv_w.shape[0] * kv_w.shape[1] * kv_w.shape[2], kv_w.shape[3])
        kv_part = lax.dot_general(
            part_tok, kv_w, (((1,), (1,)), ((), ())), preferred_element_type=jnp.float32
        )
        return q_part, kv_part

    def project(block, before):
        acc_q[...] = jnp.zeros_like(acc_q)
        acc_kv[...] = jnp.zeros_like(acc_kv)
        for chunk in range(CHUNKS):
            before(chunk)
            q_part, kv_part = products(block, pl.ds(chunk * step, step))
            acc_q[...] += q_part
            acc_kv[...] += kv_part
        finish(block, acc_q[...], acc_kv[...])

    project(z, lambda chunk: None)
    for chunk in range(CHUNKS):
        pass_on(2, chunk)
    for distance in (1, 2):

        @pl.loop(0, 2)
        def _(side):
            block = z - distance + 2 * distance * side

            @pl.when(jnp.logical_and(block >= 0, block < LINE))
            def _():
                project(block, lambda chunk: None)

    @pl.when(jnp.logical_or(z == 0, z == LINE - 1))
    def _():
        project(LINE - 1 - z, lambda chunk: pass_on(3, chunk))

    @pl.loop(0, LINE)
    def _(block):
        for copy in result_arrivals(block):
            copy.wait_recv()

    count = rows * PLANE * LINE
    low_half = lax.broadcasted_iota(jnp.int32, (count, head), 1) < head // 2
    kv_0 = kv_all[0].reshape(count, head).astype(jnp.float32)
    kv_1 = kv_all[1].reshape(count, head).astype(jnp.float32)
    key = jnp.where(low_half, kv_0, pltpu.roll(kv_1, head // 2, 1))
    value = jnp.where(low_half, pltpu.roll(kv_0, head // 2, 1), kv_1).astype(jnp.bfloat16)
    value = jnp.concatenate([value, jnp.ones_like(value)], 1)

    def turn(values, gain, where):
        scale = lax.rsqrt(jnp.mean(values * values, -1, keepdims=True) + EPS)
        normed = values * scale * gain
        return (normed * cos_t[where] + pltpu.roll(normed, head // 2, 1) * sin_t[where]).astype(jnp.bfloat16)

    everything = slice(0, count)
    query = q_all[...].reshape(count, head).astype(jnp.float32)
    q_rot = turn(query, q_gain[...], everything)
    k_rot = turn(key, k_gain[pl.ds(shared, 1), :], everything)
    tile = rows * PLANE
    factor = float(head) ** (-0.5) * 1.4426950408889634
    for i in range(LINE):
        scores = lax.dot_general(
            q_rot[i * tile : (i + 1) * tile], k_rot[: (i + 1) * tile], (((1,), (1,)), ((), ())),
            preferred_element_type=jnp.float32,
        )
        weights = jnp.exp2(scores * factor)
        at_row = i * tile + lax.broadcasted_iota(jnp.int32, scores.shape, 0)
        at_col = lax.broadcasted_iota(jnp.int32, scores.shape, 1)
        weights = jnp.where(at_col <= at_row, weights, 0.0).astype(jnp.bfloat16)
        total = jnp.dot(weights, value[: (i + 1) * tile], preferred_element_type=jnp.float32)
        out[i * tile : (i + 1) * tile, :] = (total[:, :head] / total[:, head:]).astype(out.dtype)

    for chunk in range(CHUNKS):
        for block in range(LINE):

            @pl.when(jnp.logical_and(block <= z, z < LINE - 1))
            def _():
                token_copy(block, chunk, True).wait_send()

            @pl.when(jnp.logical_and(block >= z, z > 0))
            def _():
                token_copy(block, chunk, False).wait_send()

    for i in range(last_piece + 1):
        y_copy(i).wait_send()
        x_copy(i, g).wait_send()
        diag_copy(i, g).wait_send()
        diag_copy(i, 1 - g).wait_send()
    for copy in core_copies(False):
        copy.wait_send()

    @pl.loop(0, LINE)
    def _(block):
        for copy in result_copies(block):
            copy.wait_send()


def kernel_device(tokens, w_query, w_key, w_value, q_gain, k_gain):
    rows, width = tokens.shape
    head = w_query.shape[1]
    thin = w_key.shape[1]
    count = rows * lax.axis_size("row")
    half = head // 2
    freq = THETA ** (-(jnp.arange(half, dtype=jnp.float32) * 2.0 / head))
    freq = jnp.concatenate([freq, freq])[None, :]
    bf16, f32 = jnp.bfloat16, jnp.float32
    dma = pltpu.SemaphoreType.DMA
    hbm = pl.BlockSpec(memory_space=pl.ANY)
    vmem = pl.BlockSpec(memory_space=pltpu.VMEM)
    blocks = LINE * PLANE
    return pl.pallas_call(
        layer_kernel,
        out_shape=jax.ShapeDtypeStruct((count, head), bf16),
        in_specs=[hbm] * 4 + [vmem] * 3,
        out_specs=vmem,
        scratch_shapes=[
            pltpu.VMEM((LINE, rows, width), bf16),
            pltpu.VMEM((width, PLANE * head), bf16),
            pltpu.VMEM((2, PLANE, thin, width), bf16),
            pltpu.VMEM((LINE, PLANE - 1, rows, head), bf16),
            pltpu.VMEM((blocks, rows, head), bf16),
            pltpu.VMEM((2, blocks, rows, 2 * PLANE * thin), bf16),
            pltpu.VMEM((count, head), f32),
            pltpu.VMEM((count, head), f32),
            pltpu.VMEM((rows, PLANE * head), f32),
            pltpu.VMEM((rows, 2 * PLANE * thin), f32),
            dma((4,)),
            dma((LINE, CHUNKS)),
            dma((LINE, CHUNKS)),
            dma((LINE, CHUNKS)),
            dma((3,)),
            dma((3,)),
            dma((PARTS // 2 + 1,)),
            dma((PARTS // 2 + 1,)),
            dma((PARTS + 2,)),
            dma((PARTS + 2,)),
            dma((PARTS + 2,)),
            dma((LINE, 3)),
            dma((LINE, 3)),
            dma((LINE, 7)),
            dma((LINE, 7)),
        ],
        compiler_params=pltpu.CompilerParams(
            collective_id=0, has_side_effects=True, vmem_limit_bytes=48 * 1024 * 1024
        ),
    )(tokens, w_query, w_key.T, w_value.T, q_gain, k_gain, freq)


def per_device(*args):
    fits = (
        lax.axis_size("row") == LINE * PLANE
        and lax.axis_size("groups") == 2
        and args[0].shape[0] <= 64
        and args[0].shape[1] % (PARTS * 128) == 0
        and args[1].shape[1] == 128
        and args[2].shape[1] * GROUP == 128
    )
    return kernel_device(*args) if fits else gathered_device(*args)


def solution(mesh):
    in_specs = (
        P(("groups", "row"), None),
        P(None, "row"),
        P(None, "row"),
        P(None, "row"),
        P("row", None),
        P(),
    )
    out_specs = P("groups", "row")
    return jax.shard_map(
        per_device, mesh=mesh, in_specs=in_specs, out_specs=out_specs, check_vma=False
    )
```

```python
import jax
import jax.numpy as jnp
from jax import lax
from jax.experimental import pallas as pl
from jax.experimental.pallas import tpu as pltpu
from jax.sharding import PartitionSpec as P

GROUP = 8


EPS = 1e-06
THETA = 1000000.0


def swapped(block, axis, apart):
    count = lax.axis_size(axis)
    route = []
    for low in range(count):
        high = low | 1 << apart
        if high != low and high < count:
            route += [(low, high), (high, low)]
    return lax.ppermute(block, axis, route)


def rope_tables(count, width):
    half = width // 2
    freq = THETA ** (-(jnp.arange(half, dtype=jnp.float32) * 2.0 / width))
    angles = jnp.arange(count, dtype=jnp.float32)[:, None] * freq[None, :]
    cosine = jnp.cos(angles)
    sine = jnp.sin(angles)
    return (jnp.concatenate([cosine, cosine], 1), jnp.concatenate([sine, sine], 1))


def norm_rope(raw, gain, cosine, sine):
    values = raw.astype(jnp.float32)
    scale = lax.rsqrt(jnp.mean(values * values, -1, keepdims=True) + EPS)
    normed = values * scale * gain
    half = normed.shape[-1] // 2
    turned = jnp.concatenate([-normed[:, half:], normed[:, :half]], 1)
    return (normed * cosine + turned * sine).astype(jnp.bfloat16)


def attend(query, start, key, value):
    width = query.shape[1]
    scores = jnp.dot(query, key.T, preferred_element_type=jnp.float32) * float(width) ** (-0.5)
    rows = start + lax.broadcasted_iota(jnp.int32, scores.shape, 0)
    cols = lax.broadcasted_iota(jnp.int32, scores.shape, 1)
    scores = jnp.where(cols <= rows, scores, jnp.float32(-1e30))
    top = jnp.max(scores, -1, keepdims=True)
    weights = jnp.exp(scores - top)
    total = jnp.sum(weights, -1, keepdims=True)
    probs = (weights / total).astype(jnp.bfloat16)
    return jnp.dot(probs, value, preferred_element_type=jnp.float32).astype(jnp.bfloat16)


def order_pair(mine, other, upper):
    lower_part = jnp.where(upper, other, mine)
    upper_part = jnp.where(upper, mine, other)
    return jnp.concatenate([lower_part, upper_part], 1)


def gathered_device(tokens, w_query, w_key, w_value, q_gain, k_gain):
    devices = lax.axis_size("row")
    owner = lax.axis_index("row")
    head_size = w_query.shape[1]
    count = tokens.shape[0] * devices
    shared = owner // GROUP
    levels = GROUP.bit_length() - 1
    merged = jnp.concatenate([w_query, w_key, w_value], 1)
    projected = jnp.dot(
        lax.all_gather(tokens, "row", axis=0, tiled=True),
        merged,
        preferred_element_type=jnp.float32,
    ).astype(jnp.bfloat16)
    query = projected[:, :head_size]
    key_cols = w_key.shape[1]
    key = projected[:, head_size : head_size + key_cols]
    value = projected[:, head_size + key_cols :]
    for level in range(levels):
        k_other, v_other = swapped((key, value), "row", level)
        upper = owner >> level & 1 == 1
        key = order_pair(key, k_other, upper)
        value = order_pair(value, v_other, upper)
    cosine, sine = rope_tables(count, head_size)
    q_rot = norm_rope(query, q_gain, cosine, sine)
    k_rot = norm_rope(key, lax.dynamic_slice_in_dim(k_gain, shared, 1, 0), cosine, sine)
    block = min(512, count)
    outputs = []
    for index in range(count // block):
        start = index * block
        finish = start + block
        outputs.append(attend(q_rot[start:finish], start, k_rot[:finish], value[:finish]))
    return jnp.concatenate(outputs, 0)


LINE, PLANE = 4, 4
CHUNKS = 4
PARTS = 8


def layer_kernel(
    tokens, w_query, w_kv_k, w_kv_v, q_gain_in, k_gain_in, freq_in, out,
    q_gain, k_gain, freq,
    tok, wq, wkv, q_stage, q_all, kv_all, cos_t, sin_t, acc_q, acc_kv, q_rot, k_rot, value, total,
    local_sem, right_send, left_send, tok_recv,
    core_send, core_recv, y_send, x_send, w_recv, diag_send, diag_recv,
    q_send, q_recv, kv_send, kv_recv,
):
    me = lax.axis_index("row")
    g = lax.axis_index("groups")
    z, s = me // PLANE, me % PLANE
    y, c = s // 2, s % 2
    peers = [s, y * 2 + 1 - c, (1 - y) * 2 + c, (1 - y) * 2 + 1 - c]
    half = z % 2
    pair_z = z + 1 - 2 * half
    shared = z // 2
    rows, width = tokens.shape
    head = w_query.shape[1]
    step = width // CHUNKS
    part = width // PARTS

    def at(zz, ss):
        return {"row": zz * PLANE + ss}

    barrier = pltpu.get_barrier_semaphore()
    friends = [at(z, p) for p in peers[1:]] + [at(pair_z, p) for p in peers]
    friends.append({"groups": 1 - g})
    for friend in friends:
        pl.semaphore_signal(barrier, inc=1, device_id=friend)
    far_z = z - 1 + 2 * half
    has_far = jnp.logical_and(far_z >= 0, far_z < LINE)

    @pl.when(has_far)
    def _():
        pl.semaphore_signal(barrier, inc=1, device_id=at(far_z, s))

    def own(src, dst, index):
        return pltpu.make_async_copy(src, dst, local_sem.at[index])

    locals_ = [
        own(w_kv_k, wkv.at[0, s], 0),
        own(w_kv_v, wkv.at[1, s], 1),
        own(tokens, tok.at[z], 2),
        own(w_query, wq.at[:, pl.ds(0, head)], 3),
        own(q_gain_in, q_gain, 4),
        own(k_gain_in, k_gain, 5),
        own(freq_in, freq, 6),
    ]
    for copy in locals_:
        copy.start()

    pl.semaphore_wait(barrier, len(friends) + jnp.where(has_far, 1, 0))

    def remote(src, dst, send, recv, device):
        return pltpu.make_async_remote_copy(src, dst, send, recv, device_id=device)

    def token_copy(block, chunk, right, src=None):
        view = tok.at[block, :, pl.ds(chunk * step, step)]
        sems = right_send if right else left_send
        return remote(
            view if src is None else src, view, sems.at[block, chunk],
            tok_recv.at[block, chunk], at(z + 1 if right else z - 1, s),
        )

    for chunk in range(CHUNKS):
        view = tokens.at[:, pl.ds(chunk * step, step)]

        @pl.when(z > 0)
        def _():
            token_copy(z, chunk, False, view).start()

        @pl.when(z < LINE - 1)
        def _():
            token_copy(z, chunk, True, view).start()

    last_piece = PARTS // 2

    def piece(i, parity, slot):
        if i == last_piece:
            return wkv.at[parity, peers[slot]], PARTS + parity
        index = 2 * i + parity
        rows_ = pl.ds(pl.multiple_of(index * part, part), part)
        return wq.at[rows_, pl.ds(slot * head, head)], index

    def y_copy(i):
        view, index = piece(i, g, 2)
        mine, _ = piece(i, g, 0)
        if i == last_piece:
            view = mine
        return remote(mine, view, y_send.at[i], w_recv.at[index], at(z, peers[2]))

    def y_arrival(i):
        view, index = piece(i, g, 2)
        return remote(view, view, y_send.at[i], w_recv.at[index], at(z, peers[2]))

    def x_copy(i, parity):
        view, index = piece(i, parity, 2)
        return remote(view, view, x_send.at[i], w_recv.at[index], {"groups": 1 - g})

    def diag_copy(i, parity):
        view, index = piece(i, parity, 2)
        if i == last_piece:
            there = view
        else:
            there, _ = piece(i, parity, 3)
        return remote(view, there, diag_send.at[index], diag_recv.at[index], at(z, peers[1]))

    def diag_arrival(i, parity):
        view, index = piece(i, parity, 3)
        return remote(view, view, diag_send.at[index], diag_recv.at[index], at(z, peers[1]))

    def core_copies(incoming):
        whose = peers[1] if incoming else s
        cols = pl.ds(head, head)
        mine = wq.at[:, cols] if incoming else wq.at[:, pl.ds(0, head)]
        return [
            remote(wkv.at[i, whose], wkv.at[i, whose], core_send.at[i], core_recv.at[i], at(z, peers[1]))
            for i in (0, 1)
        ] + [remote(mine, wq.at[:, cols], core_send.at[2], core_recv.at[2], at(z, peers[1]))]

    for copy in locals_:
        copy.wait()
    for i in range(last_piece + 1):
        y_copy(i).start()
    for copy in core_copies(False):
        copy.start()

    spot = lax.broadcasted_iota(jnp.int32, cos_t.shape, 0).astype(jnp.float32)
    angle = spot * freq[...]
    lane = lax.broadcasted_iota(jnp.int32, cos_t.shape, 1)
    cos_t[...] = jnp.cos(angle)
    sine = jnp.sin(angle)
    sin_t[...] = jnp.where(lane < head // 2, -sine, sine)

    def pass_on(distance, chunk):
        low, high = z - distance, z + distance

        @pl.when(low >= 0)
        def _():
            token_copy(low, chunk, True).wait_recv()

            @pl.when(z < LINE - 1)
            def _():
                token_copy(low, chunk, True).start()

        @pl.when(high < LINE)
        def _():
            token_copy(high, chunk, False).wait_recv()

            @pl.when(z > 0)
            def _():
                token_copy(high, chunk, False).start()

    def take_x(i):
        x_copy(i, 1 - g).wait_recv()
        diag_copy(i, 1 - g).start()

    for i in range(last_piece + 1):
        y_arrival(i).wait_recv()
        x_copy(i, g).start()
        diag_copy(i, g).start()
        if i < CHUNKS:
            pass_on(1, i)
        if i > 0:
            take_x(i - 1)
    take_x(last_piece)
    for copy in core_copies(True):
        copy.wait_recv()
    for i in range(last_piece + 1):
        diag_arrival(i, g).wait_recv()
        diag_arrival(i, 1 - g).wait_recv()
    for i in range(last_piece + 1):
        y_copy(i).wait_send()
        x_copy(i, g).wait_send()
        diag_copy(i, g).wait_send()
        diag_copy(i, 1 - g).wait_send()
    for copy in core_copies(False):
        copy.wait_send()

    def result_copies(block):
        place = block * PLANE + s
        copies = []
        for t in (1, 2, 3):
            copies.append(remote(
                q_stage.at[block, t - 1], q_all.at[place], q_send.at[block, t - 1],
                q_recv.at[block, t - 1], at(z, peers[t]),
            ))
        for far in (0, 1):
            for t in range(PLANE):
                if far == 0 and t == 0:
                    continue
                i = far * PLANE + t - 1
                copies.append(remote(
                    kv_all.at[half, place], kv_all.at[half, place], kv_send.at[block, i],
                    kv_recv.at[block, i], at(pair_z if far else z, peers[t]),
                ))
        return copies

    def result_arrivals(block):
        arrivals = []
        for t in (1, 2, 3):
            place = q_all.at[block * PLANE + peers[t]]
            arrivals.append(remote(
                place, place, q_send.at[block, t - 1], q_recv.at[block, t - 1], at(z, peers[t]),
            ))
        for far in (0, 1):
            for t in range(PLANE):
                if far == 0 and t == 0:
                    continue
                i = far * PLANE + t - 1
                place = kv_all.at[1 - half if far else half, block * PLANE + peers[t]]
                arrivals.append(remote(
                    place, place, kv_send.at[block, i], kv_recv.at[block, i],
                    at(pair_z if far else z, peers[t]),
                ))
        return arrivals

    def finish(block, q_sum, kv_sum):
        q_bf = q_sum.astype(jnp.bfloat16)
        place = block * PLANE + s
        q_all[place] = q_bf[:, :head]
        for t in (1, 2, 3):
            q_stage[block, t - 1] = q_bf[:, t * head : (t + 1) * head]
        kv_all[half, place] = kv_sum.astype(jnp.bfloat16)
        for copy in result_copies(block):
            copy.start()

    def products(block, cols):
        part_tok = tok[block, :, cols]
        q_part = jnp.dot(part_tok, wq[cols, :], preferred_element_type=jnp.float32)
        kv_w = wkv[:, :, :, cols]
        kv_w = kv_w.reshape(kv_w.shape[0] * kv_w.shape[1] * kv_w.shape[2], kv_w.shape[3])
        kv_part = lax.dot_general(
            part_tok, kv_w, (((1,), (1,)), ((), ())), preferred_element_type=jnp.float32
        )
        return q_part, kv_part

    def project(block, before):
        acc_q[...] = jnp.zeros_like(acc_q)
        acc_kv[...] = jnp.zeros_like(acc_kv)
        for chunk in range(CHUNKS):
            before(chunk)
            q_part, kv_part = products(block, pl.ds(chunk * step, step))
            acc_q[...] += q_part
            acc_kv[...] += kv_part
        finish(block, acc_q[...], acc_kv[...])

    project(z, lambda chunk: None)
    for chunk in range(CHUNKS):
        pass_on(2, chunk)
    for distance in (1, 2):

        @pl.loop(0, 2)
        def _(side):
            block = z - distance + 2 * distance * side

            @pl.when(jnp.logical_and(block >= 0, block < LINE))
            def _():
                project(block, lambda chunk: None)

    count = rows * PLANE * LINE
    tile = rows * PLANE
    lower = z < LINE // 2
    last = jnp.where(lower, LINE - 1, 0)
    factor = float(head) ** (-0.5) * 1.4426950408889634

    def turn(values, gain, where):
        scale = lax.rsqrt(jnp.mean(values * values, -1, keepdims=True) + EPS)
        normed = values * scale * gain
        return (normed * cos_t[where, :] + pltpu.roll(normed, head // 2, 1) * sin_t[where, :]).astype(jnp.bfloat16)

    def take(block):
        for copy in result_arrivals(block):
            copy.wait_recv()
        where = pl.ds(pl.multiple_of(block * tile, tile), tile)
        places = pl.ds(block * PLANE, PLANE)
        low_half = lax.broadcasted_iota(jnp.int32, (tile, head), 1) < head // 2
        kv_0 = kv_all[0, places].reshape(tile, head).astype(jnp.float32)
        kv_1 = kv_all[1, places].reshape(tile, head).astype(jnp.float32)
        key = jnp.where(low_half, kv_0, pltpu.roll(kv_1, head // 2, 1))
        val = jnp.where(low_half, pltpu.roll(kv_0, head // 2, 1), kv_1).astype(jnp.bfloat16)
        value[where, :head] = val
        value[where, head:] = jnp.ones_like(val)
        query = q_all[places].reshape(tile, head).astype(jnp.float32)
        q_rot[where, :] = turn(query, q_gain[...], where)
        k_rot[where, :] = turn(key, k_gain[pl.ds(shared, 1), :], where)

    def attend_part(first, stop, key_first, key_stop):
        scores = lax.dot_general(
            q_rot[first:stop, :], k_rot[key_first:key_stop, :], (((1,), (1,)), ((), ())),
            preferred_element_type=jnp.float32,
        )
        weights = jnp.exp2(scores * factor)
        if key_stop > first:
            at_row = first + lax.broadcasted_iota(jnp.int32, scores.shape, 0)
            at_col = key_first + lax.broadcasted_iota(jnp.int32, scores.shape, 1)
            weights = jnp.where(at_col <= at_row, weights, 0.0)
        return jnp.dot(
            weights.astype(jnp.bfloat16), value[key_first:key_stop, :], preferred_element_type=jnp.float32
        )

    def store(first, stop, sums):
        out[first:stop, :] = (sums[:, :head] / sums[:, head:]).astype(out.dtype)

    @pl.loop(0, LINE - 1)
    def _(i):
        block = i + 1 - jnp.where(lower, 1, 0)
        take(block)
        for copy in result_copies(block):
            copy.wait_send()

    @pl.when(lower)
    def _():
        for i in range(LINE - 1):
            store(i * tile, (i + 1) * tile, attend_part(i * tile, (i + 1) * tile, 0, (i + 1) * tile))

    @pl.when(jnp.logical_not(lower))
    def _():
        for i in range(1, LINE):
            total[i * tile : (i + 1) * tile, :] = attend_part(i * tile, (i + 1) * tile, tile, (i + 1) * tile)

    for chunk in range(CHUNKS):
        for block in range(LINE):

            @pl.when(jnp.logical_and(block <= z, z < LINE - 1))
            def _():
                token_copy(block, chunk, True).wait_send()

            @pl.when(jnp.logical_and(block >= z, z > 0))
            def _():
                token_copy(block, chunk, False).wait_send()

    @pl.when(jnp.logical_or(z == 0, z == LINE - 1))
    def _():
        project(LINE - 1 - z, lambda chunk: pass_on(3, chunk))

    take(last)

    @pl.when(lower)
    def _():
        store(count - tile, count, attend_part(count - tile, count, 0, count))

    @pl.when(jnp.logical_not(lower))
    def _():
        store(0, tile, attend_part(0, tile, 0, tile))
        for i in range(1, LINE):
            first, stop = i * tile, (i + 1) * tile
            store(first, stop, total[first:stop, :] + attend_part(first, stop, 0, tile))

    for copy in result_copies(last):
        copy.wait_send()


def kernel_device(tokens, w_query, w_key, w_value, q_gain, k_gain):
    rows, width = tokens.shape
    head = w_query.shape[1]
    thin = w_key.shape[1]
    count = rows * lax.axis_size("row")
    half = head // 2
    freq = THETA ** (-(jnp.arange(half, dtype=jnp.float32) * 2.0 / head))
    freq = jnp.concatenate([freq, freq])[None, :]
    bf16, f32 = jnp.bfloat16, jnp.float32
    dma = pltpu.SemaphoreType.DMA
    hbm = pl.BlockSpec(memory_space=pltpu.HBM)
    vmem = pl.BlockSpec(memory_space=pltpu.VMEM)
    blocks = LINE * PLANE
    return pl.pallas_call(
        layer_kernel,
        out_shape=jax.ShapeDtypeStruct((count, head), bf16),
        in_specs=[hbm] * 7,
        out_specs=vmem,
        scratch_shapes=[
            pltpu.VMEM(q_gain.shape, f32),
            pltpu.VMEM(k_gain.shape, f32),
            pltpu.VMEM(freq.shape, f32),
            pltpu.VMEM((LINE, rows, width), bf16),
            pltpu.VMEM((width, PLANE * head), bf16),
            pltpu.VMEM((2, PLANE, thin, width), bf16),
            pltpu.VMEM((LINE, PLANE - 1, rows, head), bf16),
            pltpu.VMEM((blocks, rows, head), bf16),
            pltpu.VMEM((2, blocks, rows, 2 * PLANE * thin), bf16),
            pltpu.VMEM((count, head), f32),
            pltpu.VMEM((count, head), f32),
            pltpu.VMEM((rows, PLANE * head), f32),
            pltpu.VMEM((rows, 2 * PLANE * thin), f32),
            pltpu.VMEM((count, head), bf16),
            pltpu.VMEM((count, head), bf16),
            pltpu.VMEM((count, 2 * head), bf16),
            pltpu.VMEM((count, 2 * head), f32),
            dma((7,)),
            dma((LINE, CHUNKS)),
            dma((LINE, CHUNKS)),
            dma((LINE, CHUNKS)),
            dma((3,)),
            dma((3,)),
            dma((PARTS // 2 + 1,)),
            dma((PARTS // 2 + 1,)),
            dma((PARTS + 2,)),
            dma((PARTS + 2,)),
            dma((PARTS + 2,)),
            dma((LINE, 3)),
            dma((LINE, 3)),
            dma((LINE, 7)),
            dma((LINE, 7)),
        ],
        compiler_params=pltpu.CompilerParams(
            collective_id=0, has_side_effects=True, vmem_limit_bytes=48 * 1024 * 1024
        ),
    )(tokens, w_query, w_key.T, w_value.T, q_gain, k_gain, freq)


def per_device(*args):
    fits = (
        lax.axis_size("row") == LINE * PLANE
        and lax.axis_size("groups") == 2
        and args[0].shape[0] <= 64
        and args[0].shape[1] % (PARTS * 128) == 0
        and args[1].shape[1] == 128
        and args[2].shape[1] * GROUP == 128
    )
    return kernel_device(*args) if fits else gathered_device(*args)


def solution(mesh):
    in_specs = (
        P(("groups", "row"), None),
        P(None, "row"),
        P(None, "row"),
        P(None, "row"),
        P("row", None),
        P(),
    )
    out_specs = P("groups", "row")
    return jax.shard_map(
        per_device, mesh=mesh, in_specs=in_specs, out_specs=out_specs, check_vma=False
    )
```

```python
import jax
import jax.numpy as jnp
from jax import lax
from jax.experimental import pallas as pl
from jax.experimental.pallas import tpu as pltpu
from jax.sharding import PartitionSpec as P

GROUP = 8


EPS = 1e-06
THETA = 1000000.0


def swapped(block, axis, apart):
    count = lax.axis_size(axis)
    route = []
    for low in range(count):
        high = low | 1 << apart
        if high != low and high < count:
            route += [(low, high), (high, low)]
    return lax.ppermute(block, axis, route)


def rope_tables(count, width):
    half = width // 2
    freq = THETA ** (-(jnp.arange(half, dtype=jnp.float32) * 2.0 / width))
    angles = jnp.arange(count, dtype=jnp.float32)[:, None] * freq[None, :]
    cosine = jnp.cos(angles)
    sine = jnp.sin(angles)
    return (jnp.concatenate([cosine, cosine], 1), jnp.concatenate([sine, sine], 1))


def norm_rope(raw, gain, cosine, sine):
    values = raw.astype(jnp.float32)
    scale = lax.rsqrt(jnp.mean(values * values, -1, keepdims=True) + EPS)
    normed = values * scale * gain
    half = normed.shape[-1] // 2
    turned = jnp.concatenate([-normed[:, half:], normed[:, :half]], 1)
    return (normed * cosine + turned * sine).astype(jnp.bfloat16)


def attend(query, start, key, value):
    width = query.shape[1]
    scores = jnp.dot(query, key.T, preferred_element_type=jnp.float32) * float(width) ** (-0.5)
    rows = start + lax.broadcasted_iota(jnp.int32, scores.shape, 0)
    cols = lax.broadcasted_iota(jnp.int32, scores.shape, 1)
    scores = jnp.where(cols <= rows, scores, jnp.float32(-1e30))
    top = jnp.max(scores, -1, keepdims=True)
    weights = jnp.exp(scores - top)
    total = jnp.sum(weights, -1, keepdims=True)
    probs = (weights / total).astype(jnp.bfloat16)
    return jnp.dot(probs, value, preferred_element_type=jnp.float32).astype(jnp.bfloat16)


def order_pair(mine, other, upper):
    lower_part = jnp.where(upper, other, mine)
    upper_part = jnp.where(upper, mine, other)
    return jnp.concatenate([lower_part, upper_part], 1)


def gathered_device(tokens, w_query, w_key, w_value, q_gain, k_gain):
    devices = lax.axis_size("row")
    owner = lax.axis_index("row")
    head_size = w_query.shape[1]
    count = tokens.shape[0] * devices
    shared = owner // GROUP
    levels = GROUP.bit_length() - 1
    merged = jnp.concatenate([w_query, w_key, w_value], 1)
    projected = jnp.dot(
        lax.all_gather(tokens, "row", axis=0, tiled=True),
        merged,
        preferred_element_type=jnp.float32,
    ).astype(jnp.bfloat16)
    query = projected[:, :head_size]
    key_cols = w_key.shape[1]
    key = projected[:, head_size : head_size + key_cols]
    value = projected[:, head_size + key_cols :]
    for level in range(levels):
        k_other, v_other = swapped((key, value), "row", level)
        upper = owner >> level & 1 == 1
        key = order_pair(key, k_other, upper)
        value = order_pair(value, v_other, upper)
    cosine, sine = rope_tables(count, head_size)
    q_rot = norm_rope(query, q_gain, cosine, sine)
    k_rot = norm_rope(key, lax.dynamic_slice_in_dim(k_gain, shared, 1, 0), cosine, sine)
    block = min(512, count)
    outputs = []
    for index in range(count // block):
        start = index * block
        finish = start + block
        outputs.append(attend(q_rot[start:finish], start, k_rot[:finish], value[:finish]))
    return jnp.concatenate(outputs, 0)


LINE, PLANE = 4, 4
CHUNKS = 4
PARTS = 8


def layer_kernel(
    tokens, w_query, w_kv_k, w_kv_v, q_gain_in, k_gain_in, out,
    q_gain, k_gain,
    tok, wq, wkv, q_stage, q_all, kv_all, cos_t, sin_t, acc_q, acc_kv, q_rot, k_rot, value, total,
    local_sem, right_send, left_send, tok_recv,
    core_send, core_recv, y_send, x_send, w_recv, diag_send, diag_recv,
    q_send, q_recv, kv_send, kv_recv, relay_send,
):
    me = lax.axis_index("row")
    g = lax.axis_index("groups")
    z, s = me // PLANE, me % PLANE
    y, c = s // 2, s % 2
    peers = [s, y * 2 + 1 - c, (1 - y) * 2 + c, (1 - y) * 2 + 1 - c]
    half = z % 2
    pair_z = z + 1 - 2 * half
    shared = z // 2
    rows, width = tokens.shape
    head = w_query.shape[1]
    step = width // CHUNKS
    part = width // PARTS

    def at(zz, ss):
        return {"row": zz * PLANE + ss}

    barrier = pltpu.get_barrier_semaphore()
    friends = [at(z, p) for p in peers[1:]] + [at(pair_z, p) for p in peers]
    friends.append({"groups": 1 - g})
    for friend in friends:
        pl.semaphore_signal(barrier, inc=1, device_id=friend)
    far_z = z - 1 + 2 * half
    has_far = jnp.logical_and(far_z >= 0, far_z < LINE)

    @pl.when(has_far)
    def _():
        pl.semaphore_signal(barrier, inc=1, device_id=at(far_z, s))

    def own(src, dst, index):
        return pltpu.make_async_copy(src, dst, local_sem.at[index])

    locals_ = [
        own(w_kv_k, wkv.at[0, s], 0),
        own(w_kv_v, wkv.at[1, s], 1),
        own(tokens, tok.at[z], 2),
        own(w_query, wq.at[:, pl.ds(0, head)], 3),
        own(q_gain_in, q_gain, 4),
        own(k_gain_in, k_gain, 5),
    ]
    for copy in locals_:
        copy.start()

    pl.semaphore_wait(barrier, len(friends) + jnp.where(has_far, 1, 0))

    def remote(src, dst, send, recv, device):
        return pltpu.make_async_remote_copy(src, dst, send, recv, device_id=device)

    def token_copy(block, chunk, right, src=None):
        view = tok.at[block, :, pl.ds(chunk * step, step)]
        sems = right_send if right else left_send
        return remote(
            view if src is None else src, view, sems.at[block, chunk],
            tok_recv.at[block, chunk], at(z + 1 if right else z - 1, s),
        )

    for chunk in range(CHUNKS):
        view = tokens.at[:, pl.ds(chunk * step, step)]

        @pl.when(z > 0)
        def _():
            token_copy(z, chunk, False, view).start()

        @pl.when(z < LINE - 1)
        def _():
            token_copy(z, chunk, True, view).start()

    last_piece = PARTS // 2

    def piece(i, parity, slot):
        if i == last_piece:
            return wkv.at[parity, peers[slot]], PARTS + parity
        index = 2 * i + parity
        rows_ = pl.ds(pl.multiple_of(index * part, part), part)
        return wq.at[rows_, pl.ds(slot * head, head)], index

    def y_copy(i):
        view, index = piece(i, g, 2)
        mine, _ = piece(i, g, 0)
        if i == last_piece:
            view = mine
        return remote(mine, view, y_send.at[i], w_recv.at[index], at(z, peers[2]))

    def y_arrival(i):
        view, index = piece(i, g, 2)
        return remote(view, view, y_send.at[i], w_recv.at[index], at(z, peers[2]))

    def x_copy(i, parity):
        view, index = piece(i, parity, 2)
        return remote(view, view, x_send.at[i], w_recv.at[index], {"groups": 1 - g})

    def diag_copy(i, parity):
        view, index = piece(i, parity, 2)
        if i == last_piece:
            there = view
        else:
            there, _ = piece(i, parity, 3)
        return remote(view, there, diag_send.at[index], diag_recv.at[index], at(z, peers[1]))

    def diag_arrival(i, parity):
        view, index = piece(i, parity, 3)
        return remote(view, view, diag_send.at[index], diag_recv.at[index], at(z, peers[1]))

    def core_copies(incoming):
        whose = peers[1] if incoming else s
        cols = pl.ds(head, head)
        mine = wq.at[:, cols] if incoming else wq.at[:, pl.ds(0, head)]
        return [
            remote(wkv.at[i, whose], wkv.at[i, whose], core_send.at[i], core_recv.at[i], at(z, peers[1]))
            for i in (0, 1)
        ] + [remote(mine, wq.at[:, cols], core_send.at[2], core_recv.at[2], at(z, peers[1]))]

    for copy in locals_:
        copy.wait()
    for i in range(last_piece + 1):
        y_copy(i).start()
    for copy in core_copies(False):
        copy.start()

    spot = lax.broadcasted_iota(jnp.int32, cos_t.shape, 0).astype(jnp.float32)
    pair = lax.broadcasted_iota(jnp.int32, (1, head), 1) % (head // 2)
    coarse, fine = jnp.ones((1, head), jnp.float32), jnp.ones((1, head), jnp.float32)
    for i in range(1, 8):
        fine = jnp.where(pair % 8 == i, THETA ** (-2.0 * i / head), fine)
    for i in range(1, head // 16):
        coarse = jnp.where(pair // 8 == i, THETA ** (-16.0 * i / head), coarse)
    angle = spot * (coarse * fine)
    lane = lax.broadcasted_iota(jnp.int32, cos_t.shape, 1)
    cos_t[...] = jnp.cos(angle)
    sine = jnp.sin(angle)
    sin_t[...] = jnp.where(lane < head // 2, -sine, sine)

    def pass_on(distance, chunk):
        low, high = z - distance, z + distance

        @pl.when(low >= 0)
        def _():
            token_copy(low, chunk, True).wait_recv()

            @pl.when(z < LINE - 1)
            def _():
                token_copy(low, chunk, True).start()

        @pl.when(high < LINE)
        def _():
            token_copy(high, chunk, False).wait_recv()

            @pl.when(z > 0)
            def _():
                token_copy(high, chunk, False).start()

    def take_x(i):
        x_copy(i, 1 - g).wait_recv()
        diag_copy(i, 1 - g).start()

    for i in range(last_piece + 1):
        y_arrival(i).wait_recv()
        x_copy(i, g).start()
        diag_copy(i, g).start()
        if i < CHUNKS:
            pass_on(1, i)
        if i > 0:
            take_x(i - 1)
    take_x(last_piece)
    pass_on(2, 0)
    for copy in core_copies(True):
        copy.wait_recv()
    pass_on(2, 1)
    for i in range(last_piece + 1):
        diag_arrival(i, g).wait_recv()
        diag_arrival(i, 1 - g).wait_recv()
    for chunk in range(2, CHUNKS - 1):
        pass_on(2, chunk)

    def result_copies(block):
        place = block * PLANE + s
        copies = []
        for t in (1, 2, 3):
            copies.append(remote(
                q_stage.at[block, t - 1], q_all.at[place], q_send.at[block, t - 1],
                q_recv.at[block, t - 1], at(z, peers[t]),
            ))
        for far, t in ((0, 1), (0, 2), (0, 3), (1, 0)):
            i = far * PLANE + t - 1
            copies.append(remote(
                kv_all.at[half, place], kv_all.at[half, place], kv_send.at[block, i],
                kv_recv.at[block, i], at(pair_z if far else z, peers[t]),
            ))
        return copies

    def wide_copies(block):
        place = kv_all.at[half, block * PLANE + s]
        return [
            remote(place, place, kv_send.at[block, PLANE + t - 1], kv_recv.at[block, PLANE + t - 1], at(pair_z, peers[t]))
            for t in (1, 2, 3)
        ]

    def relay_copies(block):
        place = kv_all.at[1 - half, block * PLANE + s]
        return [
            remote(place, place, relay_send.at[block, t - 1], kv_recv.at[block, PLANE + t - 1], at(z, peers[t]))
            for t in (1, 2, 3)
        ]

    def far_arrival(block):
        place = kv_all.at[1 - half, block * PLANE + s]
        return remote(place, place, kv_send.at[block, PLANE - 1], kv_recv.at[block, PLANE - 1], at(pair_z, s))

    edge = jnp.logical_or(z == 0, z == LINE - 1)

    def relay(block):
        @pl.when(edge)
        def _():
            far_arrival(block).wait_recv()
            for copy in relay_copies(block):
                copy.start()

    def wait_results(block):
        for copy in result_copies(block):
            copy.wait_send()

        @pl.when(edge)
        def _():
            for copy in wide_copies(block) + relay_copies(block):
                copy.wait_send()

    def result_arrivals(block):
        arrivals = []
        for t in (1, 2, 3):
            place = q_all.at[block * PLANE + peers[t]]
            arrivals.append(remote(
                place, place, q_send.at[block, t - 1], q_recv.at[block, t - 1], at(z, peers[t]),
            ))
        for far in (0, 1):
            for t in (1, 2, 3):
                i = far * PLANE + t - 1
                place = kv_all.at[1 - half if far else half, block * PLANE + peers[t]]
                arrivals.append(remote(
                    place, place, kv_send.at[block, i], kv_recv.at[block, i],
                    at(pair_z if far else z, peers[t]),
                ))
        return arrivals

    def finish(block, q_sum, kv_sum):
        q_bf = q_sum.astype(jnp.bfloat16)
        place = block * PLANE + s
        q_all[place] = q_bf[:, :head]
        for t in (1, 2, 3):
            q_stage[block, t - 1] = q_bf[:, t * head : (t + 1) * head]
        kv_all[half, place] = kv_sum.astype(jnp.bfloat16)
        for copy in result_copies(block):
            copy.start()

        @pl.when(edge)
        def _():
            for copy in wide_copies(block):
                copy.start()

    def products(block, cols):
        part_tok = tok[block, :, cols]
        q_part = jnp.dot(part_tok, wq[cols, :], preferred_element_type=jnp.float32)
        kv_w = wkv[:, :, :, cols]
        kv_w = kv_w.reshape(kv_w.shape[0] * kv_w.shape[1] * kv_w.shape[2], kv_w.shape[3])
        kv_part = lax.dot_general(
            part_tok, kv_w, (((1,), (1,)), ((), ())), preferred_element_type=jnp.float32
        )
        return q_part, kv_part

    def project(block, before):
        acc_q[...] = jnp.zeros_like(acc_q)
        acc_kv[...] = jnp.zeros_like(acc_kv)
        for chunk in range(CHUNKS):
            before(chunk)
            q_part, kv_part = products(block, pl.ds(chunk * step, step))
            acc_q[...] += q_part
            acc_kv[...] += kv_part
        finish(block, acc_q[...], acc_kv[...])

    project(z, lambda chunk: None)
    pass_on(2, CHUNKS - 1)
    for distance in (1, 2):

        @pl.loop(0, 2)
        def _(side):
            block = z - distance + 2 * distance * side

            @pl.when(jnp.logical_and(block >= 0, block < LINE))
            def _():
                project(block, lambda chunk: None)

    @pl.when(jnp.logical_or(z == 0, z == LINE - 1))
    def _():
        project(LINE - 1 - z, lambda chunk: pass_on(3, chunk))

    count = rows * PLANE * LINE
    tile = rows * PLANE
    lower = z < LINE // 2
    last = jnp.where(lower, LINE - 1, 0)
    factor = float(head) ** (-0.5) * 1.4426950408889634

    def turn(values, gain, where):
        scale = lax.rsqrt(jnp.mean(values * values, -1, keepdims=True) + EPS)
        normed = values * scale * gain
        return (normed * cos_t[where, :] + pltpu.roll(normed, head // 2, 1) * sin_t[where, :]).astype(jnp.bfloat16)

    def take(block):
        for copy in result_arrivals(block):
            copy.wait_recv()

        @pl.when(jnp.logical_not(edge))
        def _():
            far_arrival(block).wait_recv()

        where = pl.ds(pl.multiple_of(block * tile, tile), tile)
        places = pl.ds(block * PLANE, PLANE)
        low_half = lax.broadcasted_iota(jnp.int32, (tile, head), 1) < head // 2
        kv_0 = kv_all[0, places].reshape(tile, head).astype(jnp.float32)
        kv_1 = kv_all[1, places].reshape(tile, head).astype(jnp.float32)
        key = jnp.where(low_half, kv_0, pltpu.roll(kv_1, head // 2, 1))
        val = jnp.where(low_half, pltpu.roll(kv_0, head // 2, 1), kv_1).astype(jnp.bfloat16)
        value[where, :head] = val
        value[where, head:] = jnp.ones_like(val)
        query = q_all[places].reshape(tile, head).astype(jnp.float32)
        q_rot[where, :] = turn(query, q_gain[...], where)
        k_rot[where, :] = turn(key, k_gain[pl.ds(shared, 1), :], where)

    def attend_part(first, stop, key_first, key_stop):
        scores = lax.dot_general(
            q_rot[first:stop, :], k_rot[key_first:key_stop, :], (((1,), (1,)), ((), ())),
            preferred_element_type=jnp.float32,
        )
        weights = jnp.exp2(scores * factor)
        if key_stop > first:
            at_row = first + lax.broadcasted_iota(jnp.int32, scores.shape, 0)
            at_col = key_first + lax.broadcasted_iota(jnp.int32, scores.shape, 1)
            weights = jnp.where(at_col <= at_row, weights, 0.0)
        return jnp.dot(
            weights.astype(jnp.bfloat16), value[key_first:key_stop, :], preferred_element_type=jnp.float32
        )

    def store(first, stop, sums):
        out[first:stop, :] = (sums[:, :head] / sums[:, head:]).astype(out.dtype)

    @pl.loop(0, LINE)
    def _(block):
        relay(block)

    @pl.loop(0, LINE - 1)
    def _(i):
        block = i + 1 - jnp.where(lower, 1, 0)
        take(block)
        wait_results(block)

    @pl.when(lower)
    def _():
        for i in range(LINE - 1):
            store(i * tile, (i + 1) * tile, attend_part(i * tile, (i + 1) * tile, 0, (i + 1) * tile))

    @pl.when(jnp.logical_not(lower))
    def _():
        for i in range(1, LINE):
            total[i * tile : (i + 1) * tile, :] = attend_part(i * tile, (i + 1) * tile, tile, (i + 1) * tile)

    for i in range(last_piece + 1):
        y_copy(i).wait_send()
        x_copy(i, g).wait_send()
        diag_copy(i, g).wait_send()
        diag_copy(i, 1 - g).wait_send()
    for copy in core_copies(False):
        copy.wait_send()

    for chunk in range(CHUNKS):
        for block in range(LINE):

            @pl.when(jnp.logical_and(block <= z, z < LINE - 1))
            def _():
                token_copy(block, chunk, True).wait_send()

            @pl.when(jnp.logical_and(block >= z, z > 0))
            def _():
                token_copy(block, chunk, False).wait_send()

    take(last)

    @pl.when(lower)
    def _():
        store(count - tile, count, attend_part(count - tile, count, 0, count))

    @pl.when(jnp.logical_not(lower))
    def _():
        store(0, tile, attend_part(0, tile, 0, tile))
        for i in range(1, LINE):
            first, stop = i * tile, (i + 1) * tile
            store(first, stop, total[first:stop, :] + attend_part(first, stop, 0, tile))

    wait_results(last)


def kernel_device(tokens, w_query, w_key, w_value, q_gain, k_gain):
    rows, width = tokens.shape
    head = w_query.shape[1]
    thin = w_key.shape[1]
    count = rows * lax.axis_size("row")
    bf16, f32 = jnp.bfloat16, jnp.float32
    dma = pltpu.SemaphoreType.DMA
    hbm = pl.BlockSpec(memory_space=pltpu.HBM)
    vmem = pl.BlockSpec(memory_space=pltpu.VMEM)
    blocks = LINE * PLANE
    return pl.pallas_call(
        layer_kernel,
        out_shape=jax.ShapeDtypeStruct((count, head), bf16),
        in_specs=[hbm] * 6,
        out_specs=vmem,
        scratch_shapes=[
            pltpu.VMEM(q_gain.shape, f32),
            pltpu.VMEM(k_gain.shape, f32),
            pltpu.VMEM((LINE, rows, width), bf16),
            pltpu.VMEM((width, PLANE * head), bf16),
            pltpu.VMEM((2, PLANE, thin, width), bf16),
            pltpu.VMEM((LINE, PLANE - 1, rows, head), bf16),
            pltpu.VMEM((blocks, rows, head), bf16),
            pltpu.VMEM((2, blocks, rows, 2 * PLANE * thin), bf16),
            pltpu.VMEM((count, head), f32),
            pltpu.VMEM((count, head), f32),
            pltpu.VMEM((rows, PLANE * head), f32),
            pltpu.VMEM((rows, 2 * PLANE * thin), f32),
            pltpu.VMEM((count, head), bf16),
            pltpu.VMEM((count, head), bf16),
            pltpu.VMEM((count, 2 * head), bf16),
            pltpu.VMEM((count, 2 * head), f32),
            dma((6,)),
            dma((LINE, CHUNKS)),
            dma((LINE, CHUNKS)),
            dma((LINE, CHUNKS)),
            dma((3,)),
            dma((3,)),
            dma((PARTS // 2 + 1,)),
            dma((PARTS // 2 + 1,)),
            dma((PARTS + 2,)),
            dma((PARTS + 2,)),
            dma((PARTS + 2,)),
            dma((LINE, 3)),
            dma((LINE, 3)),
            dma((LINE, 7)),
            dma((LINE, 7)),
            dma((LINE, 3)),
        ],
        compiler_params=pltpu.CompilerParams(
            collective_id=0, has_side_effects=True, vmem_limit_bytes=62 * 1024 * 1024
        ),
    )(tokens, w_query, w_key.T, w_value.T, q_gain, k_gain)


def per_device(*args):
    fits = (
        lax.axis_size("row") == LINE * PLANE
        and lax.axis_size("groups") == 2
        and args[0].shape[0] <= 64
        and args[0].shape[1] % (PARTS * 128) == 0
        and args[1].shape[1] == 128
        and args[2].shape[1] * GROUP == 128
    )
    return kernel_device(*args) if fits else gathered_device(*args)


def solution(mesh):
    in_specs = (
        P(("groups", "row"), None),
        P(None, "row"),
        P(None, "row"),
        P(None, "row"),
        P("row", None),
        P(),
    )
    out_specs = P("groups", "row")
    return jax.shard_map(
        per_device, mesh=mesh, in_specs=in_specs, out_specs=out_specs, check_vma=False
    )
```
